512 devices in a mesh: fsdp: 64 (over y, z_hi, x, core), basis: 8 (over z_lo).
Axes of the slice: x: 4, y: 4, z: 16 (z_hi: 2, z_lo: 8; z = z_hi * 8 + z_lo), core: 2. Of those that a mesh axis runs over, the one named last changes fastest.
Arguments:
- activations: bfloat16 [2048, 6144], P('basis', 'fsdp'), may hold values from -6 to 6
- hidden_grad: bfloat16 [2048, 8192], P('basis', 'fsdp'), may hold values from -0.1796875 to 0.1796875
- block_rows: int32 [16], P('basis'), may hold values from 1 to 128, 1280 in all
- basis: bfloat16 [6144, 4096], P('fsdp', 'basis'), may hold values from -0.21875 to 0.21875
- accumulated: float32 [6144, 8192], P('basis', 'fsdp'), may hold values from -3 to 3
Outputs:
- projected: float32 [6144, 8192], P('basis', 'fsdp')
The draws below stay inside these ranges and needn't reach their ends.
Inputs may be any that keep to these rules, and one draw needn't show every extreme that they name: `block_rows`: every block holds at least one routed token, and some block is full.
All inputs are finite; a program needn't handle non-finite values.
Results may differ from the reference program's by a relative error of at most 0.029.
Values may be sent and summed in bfloat16 or wider, within the bound.
No kernel may reach another device: no remote copies, remote signals or barrier semaphores. Data moves between devices by JAX's collectives and lax.ppermute only.
A program may use at most 64 MiB of HBM per device.

```python
import math
import jax
import jax.numpy as jnp
import numpy as np
from jax import lax

D = 6144
FWIN = 8192
R = 4096
BLOCK = 128
TOK_DEV = 256
TOKENS = 2048
NBLK = 16


def strengthened(result, rng, source, target, blocks, factor):
    def block_of(axis_at):
        return (jnp.arange(result.shape[axis_at]) // (result.shape[axis_at] // blocks)).reshape((-1,) + (1,) * (result.ndim - 1 - axis_at))

    one_side = jax.random.permutation(rng, blocks)[block_of(target)]
    second = (block_of(target) + blocks // 2) % blocks
    return jnp.where((block_of(source) == one_side) | (block_of(source) == second), factor * result, result)


def shard_levels(rng, shape, split, smallest, top_value):
    factor_of = 1.0
    for dim, shards_of in split:
        steps = jax.random.uniform(jax.random.fold_in(jax.random.fold_in(rng, 6), dim), (shards_of,), jnp.float32, smallest / len(split), top_value / len(split))
        factor_of = factor_of * jnp.repeat(jnp.exp(steps), shape[dim] // shards_of).reshape((-1,) + (1,) * (len(shape) - 1 - dim))
    return factor_of


def split_up(count, total, bound, skew):
    loads = [(1 << 20) // math.isqrt(standing ** skew) + 1 for standing in range(2, count + 1)]
    surplus, given = total - bound - (count - 1), [1] * (count - 1)
    while surplus > 0:
        movable = [i for i in range(count - 1) if given[i] < bound]
        whole, remaining = sum([loads[i] for i in movable]), surplus
        for i in movable:
            more = min(bound - given[i], max(1, remaining * loads[i] // whole), surplus)
            given[i] = given[i] + more
            surplus = surplus - more
    return np.array([bound] + given)


def uneven(stream_key, number_of, total, limit, skew):
    if number_of == 2:
        one = jax.random.randint(stream_key, (), max(1, total - limit), min(limit, total - 1) + 1)
        return jnp.stack([one, total - one])
    tallies = jnp.asarray(split_up(number_of, total, limit, skew), jnp.int32)
    couples = (number_of - 1) // 2
    source_of, receiver = tallies[1:1 + 2 * couples:2], tallies[2:2 + 2 * couples:2]
    margin = jnp.minimum(source_of - 1, limit - receiver)
    passed = jax.random.randint(jax.random.fold_in(stream_key, 1), (couples,), 0, 1 << 20) % (margin + 1)
    tallies = tallies.at[1:1 + 2 * couples:2].set(source_of - passed).at[2:2 + 2 * couples:2].set(receiver + passed)
    return tallies[jax.random.permutation(jax.random.fold_in(stream_key, 2), number_of)]


def scatter_about(key, dims, scale, limit, split=(), held_as=jnp.bfloat16):
    drawn = jax.random.normal(key, dims, jnp.float32) * scale
    if len(split) > 0:
        drawn = shard_levels(key, dims, split, -0.22, 0.18) * drawn
    return jnp.clip(drawn, min=-limit, max=limit).astype(held_as)


def noise_with(own_key, extent, spread, bound, pieces, heavy, held_as=jnp.bfloat16):
    array = spread * jax.random.normal(own_key, extent, jnp.float32)
    if pieces:
        array = array * shard_levels(own_key, extent, pieces, -0.22, 0.18)
    return jnp.clip(strengthened(array, jax.random.fold_in(own_key, 3), *heavy), -bound, bound).astype(held_as)


def setup_inputs(seed: int = 0) -> dict:
    streams_of = jax.random.split(jax.random.key(seed), 6)
    return {
        "activations": scatter_about(streams_of[0], (TOKENS, D), 1.0, 6.0, ((0, 8), (1, 64))),
        "hidden_grad": scatter_about(streams_of[1], (TOKENS, FWIN), 0.03, 0.1796875, ((0, 8), (1, 64))),
        "block_rows": uneven(streams_of[2], NBLK, 5 * NBLK * BLOCK // 8, BLOCK, 1).astype(jnp.int32),
        "basis": noise_with(streams_of[3], (D, R), D ** -0.5, 0.21875, ((0, 64), (1, 8)), (1, 0, 64, 4.0)),
        "accumulated": scatter_about(streams_of[4], (D, FWIN), 0.5, 3.0, ((0, 8), (1, 64)), jnp.float32),
    }


def reference(activations, hidden_grad, block_rows, basis, accumulated):
    tokens = activations.shape[0]
    width = activations.shape[1]
    hidden = hidden_grad.shape[1]
    position = jnp.arange(tokens, dtype=jnp.int32)
    fill_count = block_rows[(position // BLOCK).astype(jnp.int32)]
    live_rows = (position % BLOCK) < fill_count
    masked = jnp.where(live_rows[:, None], hidden_grad, jnp.zeros_like(hidden_grad))
    groups = tokens // TOK_DEV
    act_groups = activations.reshape(groups, TOK_DEV, width)
    grad_groups = masked.reshape(groups, TOK_DEV, hidden)
    acc_rows = width // groups
    acc_groups = accumulated.reshape(groups, acc_rows, hidden)
    group_ids = jnp.arange(groups, dtype=jnp.int32)

    def add_group(running, quad):
        act_part, grad_part, acc_part, group_id = quad
        term = lax.dot_general(act_part, grad_part, (((0,), (0,)), ((), ())), preferred_element_type=jnp.float32)
        row_start = (group_id * acc_rows).astype(jnp.int32)
        current = lax.dynamic_slice_in_dim(term, row_start, acc_rows, 0)
        term = lax.dynamic_update_slice_in_dim(term, current + acc_part, row_start, 0)
        term = lax.optimization_barrier(term.astype(jnp.bfloat16))
        return running + term.astype(jnp.float32), None

    start_sum = jnp.zeros((width, hidden), jnp.float32)
    grad_sum, unused = lax.scan(add_group, start_sum, (act_groups, grad_groups, acc_groups, group_ids))
    gradient = grad_sum.astype(jnp.bfloat16)
    coeffs = lax.dot_general(basis, gradient, (((0,), (0,)), ((), ())), preferred_element_type=jnp.float32).astype(jnp.bfloat16)
    col_count = basis.shape[1] // groups
    basis_stack = jnp.transpose(basis.reshape(width, groups, col_count), (1, 0, 2))
    coeff_stack = coeffs.reshape(groups, col_count, hidden)

    def add_removal(running, pair):
        basis_part, coeff_part = pair
        term = jnp.dot(basis_part, coeff_part, preferred_element_type=jnp.float32)
        term = lax.optimization_barrier(term.astype(jnp.bfloat16))
        return running + term.astype(jnp.float32), None

    removed, unused_two = lax.scan(add_removal, jnp.zeros((width, hidden), jnp.float32), (basis_stack, coeff_stack))
    return gradient.astype(jnp.float32) - removed
```

```python
import jax
import jax.numpy as jnp
from jax import lax
from jax.sharding import Mesh, PartitionSpec as P

BLOCK = 128
SIZES = {"y": 4, "half": 2, "x": 4, "core": 2, "z": 8}


def routed(value, axes, target):
    sizes = [SIZES[a] for a in axes]
    pairs = []
    coords = [()]
    for s in sizes:
        coords = [c + (i,) for c in coords for i in range(s)]
    flat = {c: i for i, c in enumerate(coords)}
    for c in coords:
        pairs.append((flat[c], flat[tuple(target(*c))]))
    return lax.ppermute(value, axes, pairs)


def swap_z(value, bit):
    return routed(value, ("z",), lambda z: (z ^ bit,))


def swap_core(value):
    return routed(value, ("core",), lambda c: (1 - c,))


def ordered(flag, first, second, axis):
    return jnp.concatenate(
        [jnp.where(flag, second, first), jnp.where(flag, first, second)], axis=axis
    )


def masked_grad(hidden_grad, block_rows):
    tokens, width = hidden_grad.shape
    position = lax.broadcasted_iota(jnp.int32, (BLOCK, width), 0)
    parts = [
        jnp.where(
            position < block_rows[i], hidden_grad[i * BLOCK : (i + 1) * BLOCK], 0
        ).astype(hidden_grad.dtype)
        for i in range(tokens // BLOCK)
    ]
    return jnp.concatenate(parts, axis=0)


def on_device(activations, hidden_grad, block_rows, basis, accumulated):
    half, core, z = lax.axis_index("half"), lax.axis_index("core"), lax.axis_index("z")
    f32, bf16 = jnp.float32, jnp.bfloat16
    rows, width = accumulated.shape

    def basis_target(s):
        def target(y, h, z):
            m = z & 3
            return (
                (((y & 1) ^ (m >> 1)) << 1) | (h ^ (m & 1)),
                (z >> 2) ^ s,
                ((y >> 1) << 2) | m,
            )

        return target

    axes = ("y", "half", "z")
    b0 = routed(basis, axes, basis_target(0))
    b1 = routed(basis, axes, basis_target(1))
    strip = ordered(half == 1, b0, b1, 1)
    panel = lax.all_gather(strip, ("y", "x", "core"), axis=0, tiled=True)

    def act_target(s):
        return lambda y, h, z: ((z >> 1) ^ y, (z & 1) ^ s, 2 * y + h)

    act_t = activations.T
    a0 = routed(act_t, axes, act_target(0))
    a1 = routed(act_t, axes, act_target(1))
    act_strip = ordered((half ^ (z & 1)) == 1, a0, a1, 1)
    act_all = lax.all_to_all(
        jnp.broadcast_to(act_strip, (16,) + act_strip.shape), ("y", "x"), 0, 0
    )
    act_all = act_all.reshape(4, -1, act_strip.shape[1])

    grad = masked_grad(hidden_grad, block_rows)
    g = jnp.stack([grad, swap_z(grad, 4)], axis=0)
    g = jnp.stack([g, swap_z(g, 2)], axis=1)
    g = jnp.stack([g, swap_z(g, 1)], axis=2)
    g = g.reshape(4, -1, width)
    g_other = swap_core(g)

    def product(right):
        total = jnp.zeros((act_all.shape[1], width), f32)
        for i in range(4):
            total = total + jnp.dot(act_all[i], right[i], preferred_element_type=f32)
        return total.reshape(4, 1, -1, width)

    theirs = swap_core(product(g_other))
    mine = product(g)
    gradient = ordered(core == 1, mine, theirs, 1).reshape(rows, width) + accumulated
    gradient = gradient.astype(bf16)

    wide = jnp.stack([gradient, swap_z(gradient, 2)], axis=0)
    wide = jnp.stack([wide, swap_z(wide, 1)], axis=1).reshape(4 * rows, width)

    coeffs = lax.dot_general(
        panel, wide, (((0,), (0,)), ((), ())), preferred_element_type=f32
    )
    coeffs = (coeffs + swap_z(coeffs.astype(bf16), 4).astype(f32)).astype(bf16)
    removal = jnp.dot(panel, coeffs, preferred_element_type=f32)
    removal = removal.reshape(2, 2, rows, width)
    kept = removal[:, 0] + swap_z(removal[:, 1].astype(bf16), 1).astype(f32)
    removed = kept[0] + swap_z(kept[1].astype(bf16), 2).astype(f32)
    return gradient.astype(f32) - removed


def solution(mesh):
    grid = Mesh(mesh.devices.reshape(tuple(SIZES.values())), tuple(SIZES))
    fsdp = ("y", "half", "x", "core")
    placed = (P("z", fsdp), P("z", fsdp), P("z"), P(fsdp, "z"), P("z", fsdp))
    return jax.shard_map(
        on_device, mesh=grid, in_specs=placed, out_specs=P("z", fsdp), check_vma=False
    )
```

```python
import jax
import jax.numpy as jnp
from jax import lax
from jax.sharding import Mesh, PartitionSpec as P

BLOCK = 128
SIZES = {"y": 4, "half": 2, "x": 4, "core": 2, "z": 8}
PAIR, FAR, NEAR = 1, 2, 0
ROUTE = ("y", "half", "z")


def bit(value, i):
    return (value >> i) & 1


def routed(value, axes, target):
    coords = [()]
    for a in axes:
        coords = [c + (i,) for c in coords for i in range(SIZES[a])]
    flat = {c: i for i, c in enumerate(coords)}
    return lax.ppermute(value, axes, [(flat[c], flat[tuple(target(*c))]) for c in coords])


def swap_z(value, i):
    return routed(value, ("z",), lambda z: (z ^ (1 << i),))


def swap_core(value):
    return routed(value, ("core",), lambda c: (1 - c,))


def basis_target(s):
    def target(y, h, z):
        b = 2 * y + h
        plane = (z & ~(1 << PAIR)) | (bit(b, PAIR) << PAIR)
        slot = b ^ plane
        return 2 * bit(slot, FAR) + bit(slot, NEAR), bit(z, PAIR) ^ s, plane

    return target


def act_target(s):
    return lambda y, h, z: ((z >> 1) ^ y, (z & 1) ^ s, 2 * y + h)


def ordered(flag, first, second, axis):
    return jnp.concatenate(
        [jnp.where(flag, second, first), jnp.where(flag, first, second)], axis=axis
    )


def masked_grad(hidden_grad, block_rows):
    tokens, width = hidden_grad.shape
    position = lax.broadcasted_iota(jnp.int32, (BLOCK, width), 0)
    parts = [
        jnp.where(
            position < block_rows[i], hidden_grad[i * BLOCK : (i + 1) * BLOCK], 0
        ).astype(hidden_grad.dtype)
        for i in range(tokens // BLOCK)
    ]
    return jnp.concatenate(parts, axis=0)


def spread(strip):
    copies = jnp.broadcast_to(strip, (16,) + strip.shape)
    return lax.all_to_all(copies, ("y", "x"), 0, 0)


def on_device(activations, hidden_grad, block_rows, basis, accumulated):
    half, core, z = lax.axis_index("half"), lax.axis_index("core"), lax.axis_index("z")
    f32, bf16 = jnp.float32, jnp.bfloat16
    rows, width = accumulated.shape
    fence = lax.optimization_barrier

    act_t = activations.T
    a0, a1 = (routed(act_t, ROUTE, act_target(s)) for s in (0, 1))
    grad = masked_grad(hidden_grad, block_rows)
    g4 = swap_z(grad, 2)
    b0, b1 = (routed(basis, ROUTE, basis_target(s)) for s in (0, 1))

    act_strip = ordered((half ^ (z & 1)) == 1, a0, a1, 1)
    act_strip, grad, g4 = fence((act_strip, grad, g4))
    act_all = spread(act_strip).reshape(4, -1, act_strip.shape[1])
    g = jnp.stack([grad, g4], axis=0)
    g = jnp.stack([g, swap_z(g, 1)], axis=1)
    g = jnp.stack([g, swap_z(g, 0)], axis=2)
    g = g.reshape(4, -1, width)

    strip = ordered(half == 1, b0, b1, 1)
    act_all, strip, g = fence((act_all, strip, g))
    g_other = swap_core(g)
    panel = spread(strip).reshape(-1, strip.shape[1])

    def product(right):
        total = jnp.zeros((act_all.shape[1], width), f32)
        for i in range(4):
            total = total + jnp.dot(act_all[i], right[i], preferred_element_type=f32)
        return total

    theirs = swap_core(product(g_other))
    mine = product(g)
    split = accumulated.reshape(4, 2, -1, width)
    added = ordered(core == 1, split[:, 0], split[:, 1], 0).reshape(2, -1, width)
    gradient = (jnp.stack([mine, theirs]) + added).astype(bf16)

    wide = jnp.stack([gradient, swap_z(gradient, FAR)], axis=1)
    wide, panel = fence((wide, panel))
    panel_other = swap_core(panel)
    wide = jnp.stack([wide, swap_z(wide, NEAR)], axis=2)
    wide = wide.reshape(2, -1, width)

    def project(left, right):
        return lax.dot_general(
            left, right, (((0,), (0,)), ((), ())), preferred_element_type=f32
        )

    coeffs = project(panel, wide[0]) + project(panel_other, wide[1])
    coeffs = (coeffs + swap_z(coeffs.astype(bf16), PAIR).astype(f32)).astype(bf16)
    removal = jnp.stack(
        [
            jnp.dot(p, coeffs, preferred_element_type=f32).reshape(2, 2, -1, width)
            for p in (panel, panel_other)
        ]
    )
    kept = removal[:, :, 0] + swap_z(removal[:, :, 1].astype(bf16), NEAR).astype(f32)
    removed = kept[:, 0] + swap_z(kept[:, 1].astype(bf16), FAR).astype(f32)
    result = (gradient.astype(f32) - removed).reshape(2, 4, 1, -1, width)
    return ordered(core == 1, result[0], result[1], 1).reshape(rows, width)


def solution(mesh):
    grid = Mesh(mesh.devices.reshape(tuple(SIZES.values())), tuple(SIZES))
    fsdp = ("y", "half", "x", "core")
    placed = (P("z", fsdp), P("z", fsdp), P("z"), P(fsdp, "z"), P("z", fsdp))
    return jax.shard_map(
        on_device, mesh=grid, in_specs=placed, out_specs=P("z", fsdp), check_vma=False
    )
```

```python
import jax
import jax.numpy as jnp
from jax import lax
from jax.sharding import Mesh, PartitionSpec as P

BLOCK = 128
SIZES = {"y": 4, "half": 2, "x": 4, "core": 2, "z": 8}
PAIR, FAR, NEAR = 2, 1, 0
ROUTE = ("y", "half", "z")


def bit(value, i):
    return (value >> i) & 1


def routed(value, axes, target):
    coords = [()]
    for a in axes:
        coords = [c + (i,) for c in coords for i in range(SIZES[a])]
    flat = {c: i for i, c in enumerate(coords)}
    return lax.ppermute(value, axes, [(flat[c], flat[tuple(target(*c))]) for c in coords])


def swap_z(value, i):
    return routed(value, ("z",), lambda z: (z ^ (1 << i),))


def swap_core(value):
    return routed(value, ("core",), lambda c: (1 - c,))


def basis_target(s):
    def target(y, h, z):
        b = 2 * y + h
        plane = (z & ~(1 << PAIR)) | (bit(b, PAIR) << PAIR)
        slot = b ^ plane
        return 2 * bit(slot, FAR) + bit(slot, NEAR), bit(z, PAIR) ^ s, plane

    return target


def act_target(s):
    return lambda y, h, z: ((z >> 1) ^ y, (z & 1) ^ s, 2 * y + h)


def ordered(flag, first, second, axis):
    return jnp.concatenate(
        [jnp.where(flag, second, first), jnp.where(flag, first, second)], axis=axis
    )


def masked_grad(hidden_grad, block_rows):
    tokens, width = hidden_grad.shape
    position = lax.broadcasted_iota(jnp.int32, (BLOCK, width), 0)
    parts = [
        jnp.where(
            position < block_rows[i], hidden_grad[i * BLOCK : (i + 1) * BLOCK], 0
        ).astype(hidden_grad.dtype)
        for i in range(tokens // BLOCK)
    ]
    return jnp.concatenate(parts, axis=0)


def spread(strip):
    copies = jnp.broadcast_to(strip, (16,) + strip.shape)
    return lax.all_to_all(copies, ("y", "x"), 0, 0)


def on_device(activations, hidden_grad, block_rows, basis, accumulated):
    half, core, z = lax.axis_index("half"), lax.axis_index("core"), lax.axis_index("z")
    f32, bf16 = jnp.float32, jnp.bfloat16
    rows, width = accumulated.shape
    fence = lax.optimization_barrier

    b0, b1 = (routed(basis, ROUTE, basis_target(s)) for s in (0, 1))
    act_t = activations.T
    a0, a1 = (routed(act_t, ROUTE, act_target(s)) for s in (0, 1))
    grad = masked_grad(hidden_grad, block_rows)
    g4 = swap_z(grad, 2)
    b0, b1, a0, a1, grad, g4 = fence((b0, b1, a0, a1, grad, g4))
    strip = ordered(half == 1, b0, b1, 1)
    panel = lax.all_gather(strip, ("y", "x", "core"), axis=0, tiled=True)

    act_strip = ordered((half ^ (z & 1)) == 1, a0, a1, 1)
    act_all = spread(act_strip).reshape(4, -1, act_strip.shape[1])
    g = jnp.stack([grad, g4], axis=0)
    g = jnp.stack([g, swap_z(g, 1)], axis=1)
    g = jnp.stack([g, swap_z(g, 0)], axis=2)
    g = g.reshape(4, -1, width)
    g_other = swap_core(g)
    act_all, g, g_other = fence((act_all, g, g_other))

    def product(right):
        total = jnp.zeros((act_all.shape[1], width), f32)
        for i in range(4):
            total = total + jnp.dot(act_all[i], right[i], preferred_element_type=f32)
        return total.reshape(4, 1, -1, width)

    theirs = swap_core(product(g_other))
    mine = product(g)
    gradient = ordered(core == 1, mine, theirs, 1).reshape(rows, width) + accumulated
    gradient = gradient.astype(bf16)

    wide = jnp.stack([gradient, swap_z(gradient, FAR)], axis=0)
    wide = jnp.stack([wide, swap_z(wide, NEAR)], axis=1)
    wide = wide.reshape(-1, width)

    def project(left):
        return lax.dot_general(
            left, wide, (((0,), (0,)), ((), ())), preferred_element_type=f32
        )

    removal = 0.0
    sums = []
    for part in jnp.split(panel, 2, axis=1):
        coeffs = project(part)
        sums.append((part, coeffs, swap_z(coeffs.astype(bf16), PAIR)))
    for part, coeffs, received in sums:
        coeffs = (coeffs + received.astype(f32)).astype(bf16)
        removal = removal + jnp.dot(part, coeffs, preferred_element_type=f32)
    removal = removal.reshape(2, 2, 2, rows // 2, width)
    near = [swap_z(removal[:, 1, i].astype(bf16), NEAR) for i in range(2)]
    kept = [removal[:, 0, i] + near[i].astype(f32) for i in range(2)]
    far = [swap_z(kept[i][1].astype(bf16), FAR) for i in range(2)]
    removed = [kept[i][0] + far[i].astype(f32) for i in range(2)]
    return gradient.astype(f32) - jnp.concatenate(removed, axis=0)


def solution(mesh):
    grid = Mesh(mesh.devices.reshape(tuple(SIZES.values())), tuple(SIZES))
    fsdp = ("y", "half", "x", "core")
    placed = (P("z", fsdp), P("z", fsdp), P("z"), P(fsdp, "z"), P("z", fsdp))
    return jax.shard_map(
        on_device, mesh=grid, in_specs=placed, out_specs=P("z", fsdp), check_vma=False
    )
```

```python
import jax
import jax.numpy as jnp
from jax import lax
from jax.sharding import Mesh, PartitionSpec as P

BLOCK = 128
SIZES = {"y": 4, "half": 2, "x": 4, "core": 2, "z": 8}
PAIR, FAR, NEAR = 2, 1, 0
ROUTE = ("y", "half", "z")


def bit(value, i):
    return (value >> i) & 1


def routed(value, axes, target):
    coords = [()]
    for a in axes:
        coords = [c + (i,) for c in coords for i in range(SIZES[a])]
    flat = {c: i for i, c in enumerate(coords)}
    return lax.ppermute(value, axes, [(flat[c], flat[tuple(target(*c))]) for c in coords])


def flip_z(value, mask):
    return routed(value, ("z",), lambda z: (z ^ mask,))


def swap_z(value, i):
    return flip_z(value, 1 << i)


def swap_core(value):
    return routed(value, ("core",), lambda c: (1 - c,))


def basis_target(s):
    def target(y, h, z):
        b = 2 * y + h
        plane = (z & ~(1 << PAIR)) | (bit(b, PAIR) << PAIR)
        slot = b ^ plane
        return 2 * bit(slot, FAR) + bit(slot, NEAR), bit(z, PAIR) ^ s, plane

    return target


def act_target(s):
    return lambda y, h, z: ((z >> 1) ^ y, (z & 1) ^ s, 2 * y + h)


def ordered(flag, first, second, axis):
    return jnp.concatenate(
        [jnp.where(flag, second, first), jnp.where(flag, first, second)], axis=axis
    )


def masked_grad(hidden_grad, block_rows):
    tokens, width = hidden_grad.shape
    position = lax.broadcasted_iota(jnp.int32, (BLOCK, width), 0)
    parts = [
        jnp.where(
            position < block_rows[i], hidden_grad[i * BLOCK : (i + 1) * BLOCK], 0
        ).astype(hidden_grad.dtype)
        for i in range(tokens // BLOCK)
    ]
    return jnp.concatenate(parts, axis=0)


def spread(strip):
    copies = jnp.broadcast_to(strip, (16,) + strip.shape)
    return lax.all_to_all(copies, ("y", "x"), 0, 0)


def on_device(activations, hidden_grad, block_rows, basis, accumulated):
    half, core, z = lax.axis_index("half"), lax.axis_index("core"), lax.axis_index("z")
    f32, bf16 = jnp.float32, jnp.bfloat16
    rows, width = accumulated.shape
    fence = lax.optimization_barrier

    b0, b1 = (routed(basis, ROUTE, basis_target(s)) for s in (0, 1))
    act_t = activations.T
    a0, a1 = (routed(act_t, ROUTE, act_target(s)) for s in (0, 1))
    grad = masked_grad(hidden_grad, block_rows)
    g4 = swap_z(grad, 2)
    b0, b1, a0, a1 = fence((b0, b1, a0, a1))
    strip = ordered(half == 1, b0, b1, 1)
    panel = lax.all_gather(strip, ("y", "x", "core"), axis=0, tiled=True)

    act_strip = ordered((half ^ (z & 1)) == 1, a0, a1, 1)
    act_strip, grad, g4 = fence((act_strip, grad, g4))
    act_all = spread(act_strip).reshape(4, -1, act_strip.shape[1])
    g = jnp.stack([grad, g4], axis=0)
    g = jnp.stack([g, swap_z(g, 1)], axis=1)
    g = jnp.stack([g, swap_z(g, 0)], axis=2)
    g = g.reshape(4, -1, width)
    g_other = swap_core(g)
    act_all, g, g_other = fence((act_all, g, g_other))

    def product(right):
        total = jnp.zeros((act_all.shape[1], width), f32)
        for i in range(4):
            total = total + jnp.dot(act_all[i], right[i], preferred_element_type=f32)
        return total.reshape(4, 1, -1, width)

    theirs = swap_core(product(g_other))
    mine = product(g)
    gradient = ordered(core == 1, mine, theirs, 1).reshape(rows, width) + accumulated
    gradient = gradient.astype(bf16)

    masks = [1 << NEAR, 1 << FAR, (1 << FAR) | (1 << NEAR)]
    wide = jnp.concatenate([gradient] + [flip_z(gradient, m) for m in masks], axis=0)

    def project(left):
        return lax.dot_general(
            left, wide, (((0,), (0,)), ((), ())), preferred_element_type=f32
        )

    removal = 0.0
    sums = []
    for part in jnp.split(panel, 2, axis=1):
        coeffs = project(part)
        sums.append((part, coeffs, swap_z(coeffs.astype(bf16), PAIR)))
    for part, coeffs, received in sums:
        coeffs = (coeffs + received.astype(f32)).astype(bf16)
        removal = removal + jnp.dot(part, coeffs, preferred_element_type=f32)
    removal = removal.reshape(4, rows, width)
    removed = removal[0]
    for slot, m in enumerate(masks, 1):
        removed = removed + flip_z(removal[slot].astype(bf16), m).astype(f32)
    return gradient.astype(f32) - removed


def solution(mesh):
    grid = Mesh(mesh.devices.reshape(tuple(SIZES.values())), tuple(SIZES))
    fsdp = ("y", "half", "x", "core")
    placed = (P("z", fsdp), P("z", fsdp), P("z"), P(fsdp, "z"), P("z", fsdp))
    return jax.shard_map(
        on_device, mesh=grid, in_specs=placed, out_specs=P("z", fsdp), check_vma=False
    )
```

```python
import jax
import jax.numpy as jnp
from jax import lax
from jax.sharding import Mesh, PartitionSpec as P

BLOCK = 128
SIZES = {"y": 4, "half": 2, "x": 4, "core": 2, "z": 8}
PAIR, FAR, NEAR = 2, 1, 0
ROUTE = ("y", "half", "z")


def bit(value, i):
    return (value >> i) & 1


def routed(value, axes, target):
    coords = [()]
    for a in axes:
        coords = [c + (i,) for c in coords for i in range(SIZES[a])]
    flat = {c: i for i, c in enumerate(coords)}
    return lax.ppermute(value, axes, [(flat[c], flat[tuple(target(*c))]) for c in coords])


def flip_z(value, mask):
    return routed(value, ("z",), lambda z: (z ^ mask,))


def swap_z(value, i):
    return flip_z(value, 1 << i)


def swap_core(value):
    return routed(value, ("core",), lambda c: (1 - c,))


def basis_target(s):
    def target(y, h, z):
        b = 2 * y + h
        plane = (z & ~(1 << PAIR)) | (bit(b, PAIR) << PAIR)
        slot = b ^ plane
        return 2 * bit(slot, FAR) + bit(slot, NEAR), bit(z, PAIR) ^ s, plane

    return target


def act_target(s):
    return lambda y, h, z: ((z ^ (2 * y + h)) & 3, (z >> 2) ^ s, 2 * y + h)


def ordered(flag, first, second, axis):
    return jnp.concatenate(
        [jnp.where(flag, second, first), jnp.where(flag, first, second)], axis=axis
    )


def masked_grad(hidden_grad, block_rows):
    tokens, width = hidden_grad.shape
    position = lax.broadcasted_iota(jnp.int32, (BLOCK, width), 0)
    parts = [
        jnp.where(
            position < block_rows[i], hidden_grad[i * BLOCK : (i + 1) * BLOCK], 0
        ).astype(hidden_grad.dtype)
        for i in range(tokens // BLOCK)
    ]
    return jnp.concatenate(parts, axis=0)


def spread(strip):
    copies = jnp.broadcast_to(strip, (16,) + strip.shape)
    return lax.all_to_all(copies, ("y", "x"), 0, 0)


def on_device(activations, hidden_grad, block_rows, basis, accumulated):
    half, core, z = lax.axis_index("half"), lax.axis_index("core"), lax.axis_index("z")
    f32, bf16 = jnp.float32, jnp.bfloat16
    rows, width = accumulated.shape
    fence = lax.optimization_barrier

    b0, b1 = (routed(basis, ROUTE, basis_target(s)) for s in (0, 1))
    act_t = activations.T
    a0, a1 = (routed(act_t, ROUTE, act_target(s)) for s in (0, 1))
    grad = masked_grad(hidden_grad, block_rows)
    g4 = swap_z(grad, 2)
    b0, b1, a0, a1 = fence((b0, b1, a0, a1))
    strip = ordered(half == 1, b0, b1, 1)
    panel = lax.all_gather(strip, ("y", "x", "core"), axis=0, tiled=True)

    act_strip = ordered((half ^ (z >> 2)) == 1, a0, a1, 1)
    act_strip, grad, g4 = fence((act_strip, grad, g4))
    act_all = spread(act_strip).reshape(4, -1, act_strip.shape[1])
    g = jnp.stack([grad, g4], axis=0)
    g = jnp.stack([g, swap_z(g, 1)], axis=0)
    g = jnp.stack([g, swap_z(g, 0)], axis=1)
    g = g.reshape(4, -1, width)
    g_other = swap_core(g)
    act_all, g, g_other = fence((act_all, g, g_other))

    def product(right):
        total = jnp.zeros((act_all.shape[1], width), f32)
        for i in range(4):
            total = total + jnp.dot(act_all[i], right[i], preferred_element_type=f32)
        return total.reshape(4, 1, -1, width)

    theirs = swap_core(product(g_other))
    mine = product(g)
    gradient = ordered(core == 1, mine, theirs, 1).reshape(rows, width) + accumulated
    gradient = gradient.astype(bf16)

    masks = [1 << NEAR, 1 << FAR, (1 << FAR) | (1 << NEAR)]
    wide = jnp.concatenate([gradient] + [flip_z(gradient, m) for m in masks], axis=0)

    def project(left):
        return lax.dot_general(
            left, wide, (((0,), (0,)), ((), ())), preferred_element_type=f32
        )

    removal = 0.0
    sums = []
    for part in jnp.split(panel, 2, axis=1):
        coeffs = project(part)
        sums.append((part, coeffs, swap_z(coeffs.astype(bf16), PAIR)))
    for part, coeffs, received in sums:
        coeffs = (coeffs + received.astype(f32)).astype(bf16)
        removal = removal + jnp.dot(part, coeffs, preferred_element_type=f32)
    removal = removal.reshape(4, rows, width)
    removed = removal[0]
    for slot, m in enumerate(masks, 1):
        removed = removed + flip_z(removal[slot].astype(bf16), m).astype(f32)
    return gradient.astype(f32) - removed


def solution(mesh):
    grid = Mesh(mesh.devices.reshape(tuple(SIZES.values())), tuple(SIZES))
    fsdp = ("y", "half", "x", "core")
    placed = (P("z", fsdp), P("z", fsdp), P("z"), P(fsdp, "z"), P("z", fsdp))
    return jax.shard_map(
        on_device, mesh=grid, in_specs=placed, out_specs=P("z", fsdp), check_vma=False
    )
```
